512 devices in a mesh: seq: 64 (over z, y), head: 8 (over x, core).
Axes of the slice: x: 4, y: 4, z: 16, core: 2. Of those that a mesh axis runs over, the one named last changes fastest.
Arguments:
- inner_acts: bfloat16 [16384, 8192], P('seq', 'head'), may hold values from -0.4375 to 0.4375
- out_grad: bfloat16 [16384, 8192], P('seq', 'head'), may hold values from -0.4375 to 0.4375
- write_proj: bfloat16 [16384, 128], P('seq'), may hold values from -3 to 3
- read_proj: bfloat16 [16384, 128], P('seq'), may hold values from -3 to 3
- log_decay: float32 [16384, 64], P('seq', 'head'), may hold values from -2.5 to 0, as said below
- w_in: bfloat16 [4096, 8192], P('seq', 'head'), may hold values from -0.1875 to 0.1875
Outputs:
- input_grad: bfloat16 [16384, 4096], P('seq', 'head')
- act_grad: bfloat16 [16384, 8192], P('seq', 'head')
- write_grad: float32 [16384, 128], P('seq')
- read_grad: float32 [16384, 128], P('seq')
The draws below stay inside these ranges and needn't reach their ends.
Inputs may be any that keep to these rules, and one draw needn't show every extreme that they name: `log_decay`: natural log of a decay factor of each head at each token; every entry is negative.
All inputs are finite; a program needn't handle non-finite values.
Results may differ from the reference program's by a relative error of at most 0.019.
Values may be sent and summed in bfloat16 or wider, within the bound.
A program may use at most 192 MiB of HBM per device.

```python
import jax
import jax.numpy as jnp
from jax import lax

D = 4096
STATE_HEADS = 64
P_SIZE = 128
N = 128
SPAN = 256
TOK_DEV = 256
SEQUENCE_TOKENS = 16384
N_HEAD = 8


def draw_log_decay(key, part):
    key_slow, key_rate, key_block, key_token, pivotal_position, pivotal_loss = jax.random.split(key, 6)
    share = 0.5
    slow_heads = jax.random.uniform(key_slow, (STATE_HEADS,), jnp.float32) < share
    unit_draw = jax.random.uniform(key_rate, (STATE_HEADS,), jnp.float32)
    slow_rate = jnp.exp(jnp.log(0.1 / SEQUENCE_TOKENS) + unit_draw * jnp.log(6.0))
    fast_low = jnp.log(4.0 / SEQUENCE_TOKENS)
    fast_rate = jnp.exp(fast_low + unit_draw * (jnp.log(1.0 / 30.0) - fast_low))
    head_decay_rate = jnp.where(slow_heads, slow_rate, fast_rate)
    block_count = SEQUENCE_TOKENS // TOK_DEV
    block_multiplier = jnp.exp(jax.random.uniform(key_block, (block_count, STATE_HEADS), jnp.float32, -0.6931, 0.6931))
    block_multiplier = jnp.repeat(block_multiplier, TOK_DEV, axis=0)
    token_multiplier = jnp.exp(jax.random.uniform(key_token, (SEQUENCE_TOKENS, STATE_HEADS), jnp.float32, -0.6931, 0.6931))
    surge_positions = jax.random.randint(pivotal_position, (3,), 0, SEQUENCE_TOKENS)
    surge_losses = jnp.log(jax.random.uniform(pivotal_loss, (3, STATE_HEADS), jnp.float32, 0.5, 0.8))
    agreement_flags = jnp.arange(SEQUENCE_TOKENS)[:, None] == surge_positions[None, :]
    surge_events = jnp.sum(jnp.where(agreement_flags[:, :, None], surge_losses[None, :, :], 0.0), axis=1)
    return (surge_events - head_decay_rate[None, :] * block_multiplier * token_multiplier).astype(jnp.float32)


def with_spikes(values, rng, source, target, blocks, factor):
    def block_of(position):
        return (jnp.arange(values.shape[position]) // (values.shape[position] // blocks)).reshape((-1,) + (1,) * (values.ndim - 1 - position))

    near = jax.random.permutation(rng, blocks)[block_of(target)]
    second = (block_of(target) + blocks // 2) % blocks
    return jnp.where((block_of(source) == near) | (block_of(source) == second), factor * values, values)


def steps_of(key, extent, cuts, least, high):
    def one(axis_at, blocks):
        draws = jax.random.uniform(jax.random.fold_in(jax.random.fold_in(key, 6), axis_at), (blocks,), jnp.float32, least / len(cuts), high / len(cuts))
        return jnp.repeat(jnp.exp(draws), extent[axis_at] // blocks).reshape((-1,) + (1,) * (len(extent) - axis_at - 1))

    level = one(*cuts[0])
    for cut in cuts[1:]:
        level = level * one(*cut)
    return level


def scatter_about(own_key, extent, spread, reach, pieces=(), held_as=jnp.bfloat16):
    drawn = jax.random.normal(own_key, extent, jnp.float32) * spread
    if len(pieces) > 0:
        drawn = steps_of(own_key, extent, pieces, -0.22, 0.18) * drawn
    return jnp.clip(drawn, min=-reach, max=reach).astype(held_as)


def noise_with(rng, dims, scale, most, pieces, heavy, held_as=jnp.bfloat16):
    array = scale * jax.random.normal(rng, dims, jnp.float32)
    if pieces:
        array = array * steps_of(rng, dims, pieces, -0.22, 0.18)
    return jnp.clip(with_spikes(array, jax.random.fold_in(rng, 3), *heavy), -most, most).astype(held_as)


def setup_inputs(seed: int = 0) -> dict:
    key_of = jax.random.split(jax.random.key(seed), 7)
    inner_acts = scatter_about(key_of[0], (SEQUENCE_TOKENS, STATE_HEADS * P_SIZE), 0.03, 0.4375, ((0, 64), (1, 8)))
    out_grad = scatter_about(key_of[1], (SEQUENCE_TOKENS, STATE_HEADS * P_SIZE), 0.03, 0.4375, ((0, 64), (1, 8)))
    write_proj = scatter_about(key_of[2], (SEQUENCE_TOKENS, N), 0.2, 3.0, ((0, 64),))
    read_proj = scatter_about(key_of[3], (SEQUENCE_TOKENS, N), 0.2, 3.0, ((0, 64),))
    log_decay = draw_log_decay(jax.random.fold_in(key_of[6], 71), 0)
    w_in = noise_with(key_of[5], (D, STATE_HEADS * P_SIZE), (STATE_HEADS * P_SIZE) ** -0.5, 0.1875, ((0, 64), (1, 8)), (1, 0, 64, 4.0))
    return {"inner_acts": inner_acts, "out_grad": out_grad, "write_proj": write_proj, "read_proj": read_proj, "log_decay": log_decay, "w_in": w_in}


exact_mode = lax.Precision.HIGHEST


def decay_square(cumulative):
    count = cumulative.shape[0]
    by_head = cumulative.T
    spread_log = by_head[:, :, None] - by_head[:, None, :]
    below_diag = jnp.arange(count)[:, None] >= jnp.arange(count)[None, :]
    return jnp.exp(jnp.where(below_diag[None], spread_log, -jnp.inf))


def span_terms(act_span, grad_span, log_span):
    cumulative = jnp.cumsum(log_span, axis=0)
    decays = decay_square(cumulative)
    weighted = decays * jnp.einsum('ahp,bhp->hab', grad_span, act_span, precision=exact_mode)
    return cumulative, decays, weighted


def reference(inner_acts, out_grad, write_proj, read_proj, log_decay, w_in):
    blocks = SEQUENCE_TOKENS // SPAN
    act_blocks = inner_acts.astype(jnp.float32).reshape(blocks, SPAN, STATE_HEADS, P_SIZE)
    grad_blocks = out_grad.astype(jnp.float32).reshape(blocks, SPAN, STATE_HEADS, P_SIZE)
    write_blocks = write_proj.astype(jnp.float32).reshape(blocks, SPAN, N)
    read_blocks = read_proj.astype(jnp.float32).reshape(blocks, SPAN, N)
    log_blocks = log_decay.reshape(blocks, SPAN, STATE_HEADS)
    inputs = (act_blocks, grad_blocks, write_blocks, read_blocks, log_blocks)

    def forward(state_now, block):
        act_span, grad_span, write_span, read_span, log_span = block
        cumulative, decays, weighted = span_terms(act_span, grad_span, log_span)
        local_part = jnp.einsum('hab,bn->an', weighted, write_span, precision=exact_mode)
        carried = jnp.einsum('ahp,hpn->an', grad_span * jnp.exp(cumulative)[:, :, None], state_now, precision=exact_mode)
        tail_decay = jnp.exp(cumulative[-1][None, :] - cumulative)
        new_state = jnp.exp(cumulative[-1])[:, None, None] * state_now + jnp.einsum(
            'bhp,bn->hpn', act_span * tail_decay[:, :, None], write_span, precision=exact_mode)
        return new_state, local_part + carried

    start_state = jnp.zeros((STATE_HEADS, P_SIZE, N), jnp.float32)
    unused_state, read_parts = lax.scan(forward, start_state, inputs)

    def backward(carry_grad, block):
        act_span, grad_span, write_span, read_span, log_span = block
        cumulative, decays, weighted = span_terms(act_span, grad_span, log_span)
        tail_decay = jnp.exp(cumulative[-1][None, :] - cumulative)
        scores = jnp.einsum('an,bn->ab', read_span, write_span, precision=exact_mode)
        act_local = jnp.einsum('hab,ahp->bhp', decays * scores[None], grad_span, precision=exact_mode)
        act_carry = jnp.einsum('hpn,bn->bhp', carry_grad, write_span, precision=exact_mode) * tail_decay[:, :, None]
        write_local = jnp.einsum('hab,an->bn', weighted, read_span, precision=exact_mode)
        write_carry = jnp.einsum('bhp,hpn->bn', act_span * tail_decay[:, :, None], carry_grad, precision=exact_mode)
        new_grad = jnp.exp(cumulative[-1])[:, None, None] * carry_grad + jnp.einsum(
            'ahp,an->hpn', grad_span * jnp.exp(cumulative)[:, :, None], read_span, precision=exact_mode)
        return new_grad, (act_local + act_carry, write_local + write_carry)

    unused_grad, (act_parts, write_parts) = lax.scan(backward, start_state, inputs, reverse=True)
    act_grad = act_parts.reshape(SEQUENCE_TOKENS, STATE_HEADS * P_SIZE).astype(jnp.bfloat16)
    write_grad = write_parts.reshape(SEQUENCE_TOKENS, N)
    read_grad = read_parts.reshape(SEQUENCE_TOKENS, N)
    group_cols = (STATE_HEADS // N_HEAD) * P_SIZE
    summed = jnp.zeros((SEQUENCE_TOKENS, D), jnp.float32)
    for group_idx in range(N_HEAD):
        lower_col = group_idx * group_cols
        group_term = jnp.dot(act_grad[:, lower_col:lower_col + group_cols],
                             w_in[:, lower_col:lower_col + group_cols].T,
                             preferred_element_type=jnp.float32)
        summed = summed + lax.optimization_barrier(group_term.astype(jnp.bfloat16)).astype(jnp.float32)
    return summed.astype(jnp.bfloat16), act_grad, write_grad, read_grad
```

```python
import functools

import jax
import jax.numpy as jnp
from jax import lax
from jax.experimental import pallas as pl
from jax.experimental.pallas import tpu as pltpu
from jax.sharding import PartitionSpec as P

MESH = pl.DeviceIdType.MESH
F32, BF16 = jnp.float32, jnp.bfloat16
Y = 4
T = 256
H = 8
K = 128
ROWS = 64

NN = (((1,), (0,)), ((), ()))
NT = (((1,), (1,)), ((), ()))
TN = (((0,), (0,)), ((), ()))


def dot(a, b, dims=NN):
    return lax.dot_general(a, b, dims, preferred_element_type=F32)


def remote(src, dst, send, recv, device):
    return pltpu.make_async_remote_copy(
        src, dst, send, recv, device_id=device, device_id_type=MESH
    )


def kernel(
    Z, X,
    x_ref, dy_ref, b_ref, c_ref, log_ref, w_ref,
    out_ref, act_ref, wg_ref, rg_ref,
    cs_ref, xs_ref, dys_ref, actl_ref, wt_ref,
    csall, ball, actl_all, tb_ref, atot,
    wz, up_s, up_r, dz_s, dz_r, zs, zr, cz, zin,
    g_s, g_r, st_s, st_r, act_all,
    co_s, co_r, keep, x_s, x_r, y_s, y_r,
    p_s, p_r, px, pf, pf_r, part_ref,
    y_ss, y_rs, w_ss, w_rs, z_ss, z_rs, c_ss, c_rs, x_ss, x_rs,
):
    seq, head = lax.axis_index("seq"), lax.axis_index("head")
    z, y = seq // Y, lax.rem(seq, Y)
    cx, core = head // 2, lax.rem(head, 2)

    def at_z(d):
        return (lax.rem(z + d + Z, Z) * Y + y, head)

    def y_of(d):
        return lax.rem(y + d + Y, Y)

    def at_y(d):
        return (z * Y + y_of(d), head)

    def x_of(d):
        return lax.rem(cx + d + X, X)

    def at_x(d):
        return (seq, x_of(d) * 2 + core)

    other = (seq, cx * 2 + 1 - core)

    barrier = pltpu.get_barrier_semaphore()
    partners = (
        [at_y(d) for d in range(1, Y)]
        + [at_x(d) for d in range(1, X)]
        + [other]
    )
    for device in partners:
        pl.semaphore_signal(barrier, inc=1, device_id=device, device_id_type=MESH)

    def greet(d, carry):
        pl.semaphore_signal(barrier, inc=1, device_id=at_z(d), device_id_type=MESH)
        return carry

    lax.fori_loop(1, Z, greet, 0)

    rows = lax.broadcasted_iota(jnp.int32, (T, T), 0)
    lanes = lax.broadcasted_iota(jnp.int32, (T, T), 1)
    lower = jnp.where(rows >= lanes, 1.0, 0.0).astype(F32)
    logs = jnp.concatenate([log_ref[...], jnp.zeros((T, K - H), F32)], axis=1)
    cs = lax.dot_general(
        lower, logs, NN, precision=lax.Precision.HIGHEST, preferred_element_type=F32
    )
    cs_ref[...] = cs
    cs_rows = cs.T[0:H]
    csall[y] = cs_rows
    ball[y] = b_ref[...]
    wz[z] = w_ref[...]
    tail = jnp.exp(cs[T - 1 : T] - cs)
    front = jnp.exp(cs)
    for h in range(H):
        cut = slice(h * K, (h + 1) * K)
        xs_ref[:, cut] = (x_ref[:, cut].astype(F32) * tail[:, h : h + 1]).astype(BF16)
        dys_ref[:, cut] = (dy_ref[:, cut].astype(F32) * front[:, h : h + 1]).astype(BF16)
    for i, (left, right) in enumerate(((b_ref, xs_ref), (c_ref, dys_ref))):
        total = dot(left[...], right[...], TN).astype(BF16)
        for h in range(H):
            up_s[h // 2, i, (h % 2) * K : (h % 2 + 1) * K] = total[:, h * K : (h + 1) * K]
    up_r[y] = up_s[y]

    pl.semaphore_wait(barrier, Y - 1 + X - 1 + 1 + Z - 1)

    half = Z // 2

    def w_copies(k):
        a, b = lax.rem(z - k + Z, Z), lax.rem(z + k, Z)
        if k < half - 1:
            fore, back = wz.at[a], wz.at[b]
        else:
            fore, back = wz.at[a, 0 : ROWS // 2], wz.at[b, ROWS // 2 : ROWS]
        return (
            remote(fore, fore, w_ss.at[0, k], w_rs.at[0, k], at_z(1)),
            remote(back, back, w_ss.at[1, k], w_rs.at[1, k], at_z(-1)),
        )

    def w_arrived(k):
        a, b = lax.rem(z - 1 - k + Z, Z), lax.rem(z + 1 + k, Z)
        if k < half - 1:
            fore, back = wz.at[a], wz.at[b]
        else:
            fore, back = wz.at[a, 0 : ROWS // 2], wz.at[b, ROWS // 2 : ROWS]
        remote(fore, fore, w_ss.at[0, k], w_rs.at[0, k], at_z(1)).wait_recv()
        remote(back, back, w_ss.at[1, k], w_rs.at[1, k], at_z(-1)).wait_recv()

    def w_step(k):
        if k > 0:
            w_arrived(k - 1)
        for copy in w_copies(k):
            copy.start()

    started = []

    def y_send(group, src_of, dst_of):
        for d in (2, 1, 3):
            copy = remote(
                src_of(y_of(d)), dst_of(y), y_ss.at[group, d], y_rs.at[group, d], at_y(d)
            )
            copy.start()
            started.append(copy)

    def y_wait(group, src_of, dst_of):
        for d in (1, 3, 2):
            remote(
                src_of(y_of(d)), dst_of(y_of(-d)), y_ss.at[group, d], y_rs.at[group, d], at_y(d)
            ).wait_recv()

    y_send(0, lambda t: csall.at[y], lambda s: csall.at[s])
    y_send(1, lambda t: up_s.at[t], lambda s: up_r.at[s])
    y_send(2, lambda t: ball.at[y], lambda s: ball.at[s])
    w_step(0)

    below = lanes >= rows
    scores = dot(b_ref[...], c_ref[...], NT)

    def heads(low, high):
        for h in range(low, high):
            cut = slice(h * K, (h + 1) * K)
            xh, dyh = x_ref[:, cut], dy_ref[:, cut]
            decay = jnp.exp(
                jnp.where(below, csall[y, h : h + 1, :] - cs_ref[:, h : h + 1], -jnp.inf)
            )
            weighted = decay * dot(xh, dyh, NT)
            wt_ref[...] = weighted if h == 0 else wt_ref[...] + weighted
            own = dot((decay * scores).astype(BF16), dyh)
            actl_ref[:, cut] = own
            actl_all[y, :, cut] = own.astype(BF16)

    heads(0, 4)
    y_wait(0, lambda t: csall.at[y], lambda s: csall.at[s])
    for t in range(Y):
        atot[t] = jnp.broadcast_to(csall[t][:, T - 1 : T], (H, K))

    def total_of(t, i):
        return atot[t, pl.ds(2 * y + i, 1), :]

    for i in range(2):
        plane = total_of(0, i) + total_of(1, i) + total_of(2, i) + total_of(3, i)
        dz_s[4 * i : 4 * i + 4] = jnp.broadcast_to(plane, (4, K))
    dz_r[z] = dz_s[...]

    def z_send(group, src_of, dst):
        def one(d, carry):
            t = lax.rem(z + d, Z)
            remote(
                src_of(t), dst.at[z], z_ss.at[group, d], z_rs.at[group, d], at_z(d)
            ).start()
            return carry

        lax.fori_loop(1, Z, one, 0)

    def z_wait(group, src_of, dst):
        def one(d, carry):
            remote(
                src_of(lax.rem(z + d, Z)), dst.at[lax.rem(z - d + Z, Z)],
                z_ss.at[group, d], z_rs.at[group, d], at_z(d),
            ).wait_recv()
            return carry

        lax.fori_loop(1, Z, one, 0)

    def z_sent(group, src_of, dst):
        def one(d, carry):
            remote(
                src_of(lax.rem(z + d, Z)), dst.at[z],
                z_ss.at[group, d], z_rs.at[group, d], at_z(d),
            ).wait_send()
            return carry

        lax.fori_loop(1, Z, one, 0)

    z_send(0, lambda t: dz_s, dz_r)
    w_step(1)
    heads(4, 8)
    w_step(2)

    y_wait(1, lambda t: up_s.at[t], lambda s: up_r.at[s])
    for i in range(2):
        cut = slice(i * K, (i + 1) * K)
        part = slice(i * (Z // 2), (i + 1) * (Z // 2))
        fore = up_r[0, 0, cut].astype(F32)
        back = up_r[Y - 1, 1, cut].astype(F32)
        for t in range(1, Y):
            fore = jnp.exp(total_of(t, i)) * fore + up_r[t, 0, cut].astype(F32)
            back = jnp.exp(total_of(Y - 1 - t, i)) * back + up_r[Y - 1 - t, 1, cut].astype(F32)
        zs[part, 0] = fore.astype(BF16).reshape(Z // 2, 2 * K // Z, K)
        zs[part, 1] = back.astype(BF16).reshape(Z // 2, 2 * K // Z, K)
    zr[z] = zs[z]
    z_send(1, lambda t: zs.at[t], zr)
    y_send(3, lambda t: actl_all.at[y], lambda s: actl_all.at[s])

    y_wait(2, lambda t: ball.at[y], lambda s: ball.at[s])

    def tails(t, carry):
        padded = jnp.concatenate([csall[t], jnp.zeros((K - H, T), F32)], axis=0)
        ct = padded.T
        et = jnp.exp(ct[T - 1 : T] - ct)
        bt = ball[t].astype(F32)
        for h in range(H):
            tb_ref[t, h] = (et[:, h : h + 1] * bt).astype(BF16)
        return carry

    lax.fori_loop(0, Y, tails, 0)
    wt = wt_ref[...]
    part_ref[0] = dot(wt.astype(BF16), c_ref[...])
    part_ref[1] = dot(wt.T.astype(BF16), b_ref[...])

    z_wait(0, lambda t: dz_s, dz_r)
    w_step(3)
    z_wait(1, lambda t: zs.at[t], zr)

    row = 4 * (z // (Z // 2))

    def sweep(k, carry):
        fore, back = carry
        j = Z - 1 - k
        cz[k, 0] = fore.astype(BF16)
        cz[j, 1] = back.astype(BF16)
        fore = jnp.exp(dz_r[k, pl.ds(row, 1), :]) * fore + zr[k, 0].astype(F32)
        back = jnp.exp(dz_r[j, pl.ds(row, 1), :]) * back + zr[j, 1].astype(F32)
        return fore, back

    zero = jnp.zeros((2 * K // Z, K), F32)
    lax.fori_loop(0, Z, sweep, (zero, zero))
    zin[z] = cz[z]
    z_send(2, lambda t: cz.at[t], zin)
    w_step(4)
    w_step(5)
    z_wait(2, lambda t: cz.at[t], zin)

    for i in range(2):
        cut = slice(i * K, (i + 1) * K)
        part = slice(i * (Z // 2), (i + 1) * (Z // 2))
        back = zin[part, 1].reshape(K, K).astype(F32)
        for t in reversed(range(Y)):
            g_s[t, cut] = back.astype(BF16)
            back = jnp.exp(total_of(t, i)) * back + up_r[t, 1, cut].astype(F32)
    g_r[y] = g_s[...]
    y_send(4, lambda t: g_s, lambda s: g_r.at[s])
    for i in range(2):
        cut = slice(i * K, (i + 1) * K)
        part = slice(i * (Z // 2), (i + 1) * (Z // 2))
        fore = zin[part, 0].reshape(K, K).astype(F32)
        for t in range(Y):
            st_s[t, cut] = fore.astype(BF16)
            fore = jnp.exp(total_of(t, i)) * fore + up_r[t, 0, cut].astype(F32)
    st_r[y] = st_s[y]
    y_send(5, lambda t: st_s.at[t], lambda s: st_r.at[s])
    for k in range(6, half):
        w_step(k)
    y_wait(3, lambda t: actl_all.at[y], lambda s: actl_all.at[s])
    w_arrived(half - 1)
    y_wait(4, lambda t: g_s, lambda s: g_r.at[s])
    y_wait(5, lambda t: st_s.at[t], lambda s: st_r.at[s])

    order = (2, 1, 3, 0)

    def core_copy(k):
        return remote(co_s.at[k], co_r.at[k], c_ss.at[k], c_rs.at[k], other)

    def stage_a(k):
        d = order[k]
        t = y_of(d)
        for h in range(H):
            cut = slice(h * K, (h + 1) * K)
            carried = dot(tb_ref[t, h], g_r[h // 2, t, (h % 2) * K : (h % 2 + 1) * K])
            if d == 0:
                own = (actl_ref[:, cut] + carried).astype(BF16)
                act_ref[:, cut] = own
            else:
                own = (actl_all[t, :, cut].astype(F32) + carried).astype(BF16)
            act_all[k, :, cut] = own
        act = act_all[k]
        per = Z // X
        for j in range(X):
            w = wz[per * j : per * (j + 1)].reshape(per * ROWS, H * K)
            both = dot(act, w, NT)
            low, high = both[:, 0:K], both[:, K : 2 * K]
            keep[k, j] = jnp.where(core == 0, low, high)
            co_s[k, j] = jnp.where(core == 0, high, low).astype(BF16)
        core_copy(k).start()

    def x_copies(k):
        return [
            remote(
                x_s.at[k, x_of(e)], x_r.at[k, e], x_ss.at[k, e], x_rs.at[k, e], at_x(e)
            )
            for e in range(1, X)
        ]

    def stage_b(k):
        core_copy(k).wait_recv()
        for j in range(X):
            total = keep[k, j] + co_r[k, j].astype(F32)
            keep[k, j] = total
            x_s[k, j] = total.astype(BF16)
        for copy in x_copies(k):
            copy.start()

    def y_copy(k):
        d = order[k]
        return remote(y_s.at[k], y_r.at[y], y_ss.at[6, d], y_rs.at[6, d], at_y(d))

    def stage_c(k):
        total = keep[k, cx]
        for e, copy in enumerate(x_copies(k), 1):
            copy.wait_recv()
            total = total + x_r[k, e].astype(F32)
        if order[k] == 0:
            y_r[y] = total.astype(BF16)
        else:
            y_s[k] = total.astype(BF16)
            y_copy(k).start()

    core_part = remote(p_s, p_r, c_ss.at[4], c_rs.at[4], other)
    core_total = remote(pf, pf_r, c_ss.at[5], c_rs.at[5], other)

    def parts_start():
        state = [st_r[h // 2, (h % 2) * K : (h % 2 + 1) * K] for h in range(H)]
        grad = [g_r[h // 2, y, (h % 2) * K : (h % 2 + 1) * K] for h in range(H)]
        write = part_ref[0] + dot(xs_ref[...], jnp.concatenate(grad, axis=1), NT)
        read = part_ref[1] + dot(dys_ref[...], jnp.concatenate(state, axis=1), NT)
        part_ref[0] = jnp.where(core == 0, write, read)
        p_s[...] = jnp.where(core == 0, read, write).astype(BF16)
        core_part.start()

    def part_copy(e):
        return remote(px.at[cx], px.at[cx], x_ss.at[4, e], x_rs.at[4, e], at_x(e))

    def parts_x():
        core_part.wait_recv()
        px[cx] = (part_ref[0] + p_r[...].astype(F32)).astype(BF16)
        for e in range(1, X):
            part_copy(e).start()

    def parts_core():
        for e in range(1, X):
            s = x_of(-e)
            remote(px.at[cx], px.at[s], x_ss.at[4, e], x_rs.at[4, e], at_x(e)).wait_recv()
        total = px[0].astype(F32)
        for j in range(1, X):
            total = total + px[j].astype(F32)
        pf[...] = total
        core_total.start()

    stage_a(0)
    parts_start()
    stage_a(1)
    stage_b(0)
    parts_x()
    stage_a(2)
    stage_b(1)
    stage_c(0)
    stage_a(3)
    stage_b(2)
    parts_core()
    stage_c(1)
    stage_b(3)
    stage_c(2)
    stage_c(3)
    core_total.wait_recv()
    wg_ref[...] = jnp.where(core == 0, pf[...], pf_r[...])
    rg_ref[...] = jnp.where(core == 0, pf_r[...], pf[...])
    for k in range(3):
        d = order[k]
        remote(
            y_s.at[k], y_r.at[y_of(-d)], y_ss.at[6, d], y_rs.at[6, d], at_y(d)
        ).wait_recv()
    for i in range(2):
        pieces = [y_r[t, :, i * ROWS : (i + 1) * ROWS] for t in range(Y)]
        out_ref[:, 2 * i * K : 2 * (i + 1) * K] = jnp.concatenate(pieces, axis=1)

    for copy in started:
        copy.wait_send()
    for k in range(half):
        for copy in w_copies(k):
            copy.wait_send()
    z_sent(0, lambda t: dz_s, dz_r)
    z_sent(1, lambda t: zs.at[t], zr)
    z_sent(2, lambda t: cz.at[t], zin)
    for k in range(4):
        core_copy(k).wait_send()
        for copy in x_copies(k):
            copy.wait_send()
        if order[k]:
            y_copy(k).wait_send()
    core_part.wait_send()
    core_total.wait_send()
    for e in range(1, X):
        part_copy(e).wait_send()


def solution(mesh):
    Z, X = mesh.shape["seq"] // Y, mesh.shape["head"] // 2
    piece = 2 * K // Z
    vmem, dma = pltpu.VMEM, pltpu.SemaphoreType.DMA

    def local(inner_acts, out_grad, write_proj, read_proj, log_decay, w_in):
        scratch = [
            vmem((T, K), F32),
            vmem((T, H * K), BF16),
            vmem((T, H * K), BF16),
            vmem((T, H * K), F32),
            vmem((T, T), F32),
            vmem((Y, H, T), F32),
            vmem((Y, T, K), BF16),
            vmem((Y, T, H * K), BF16),
            vmem((Y, H, T, K), BF16),
            vmem((Y, H, K), F32),
            vmem((Z, ROWS, H * K), BF16),
            vmem((Y, 2, 2 * K, K), BF16),
            vmem((Y, 2, 2 * K, K), BF16),
            vmem((8, K), F32),
            vmem((Z, 8, K), F32),
            vmem((Z, 2, piece, K), BF16),
            vmem((Z, 2, piece, K), BF16),
            vmem((Z, 2, piece, K), BF16),
            vmem((Z, 2, piece, K), BF16),
            vmem((Y, 2 * K, K), BF16),
            vmem((Y, Y, 2 * K, K), BF16),
            vmem((Y, 2 * K, K), BF16),
            vmem((Y, 2 * K, K), BF16),
            vmem((Y, T, H * K), BF16),
            vmem((Y, X, T, K), BF16),
            vmem((Y, X, T, K), BF16),
            vmem((Y, X, T, K), F32),
            vmem((Y, X, T, K), BF16),
            vmem((Y, X, T, K), BF16),
            vmem((Y, T, K), BF16),
            vmem((Y, T, K), BF16),
            vmem((T, K), BF16),
            vmem((T, K), BF16),
            vmem((X, T, K), BF16),
            vmem((T, K), F32),
            vmem((T, K), F32),
            vmem((2, T, K), F32),
            dma((7, Y)), dma((7, Y)),
            dma((2, Z // 2)), dma((2, Z // 2)),
            dma((3, Z)), dma((3, Z)),
            dma((6,)), dma((6,)),
            dma((5, X)), dma((5, X)),
        ]
        whole = pl.BlockSpec(memory_space=pltpu.VMEM)
        columns = w_in.shape[0] * mesh.shape["seq"] // mesh.shape["head"]
        return pl.pallas_call(
            functools.partial(kernel, Z, X),
            out_shape=(
                jax.ShapeDtypeStruct((T, columns), BF16),
                jax.ShapeDtypeStruct((T, H * K), BF16),
                jax.ShapeDtypeStruct((T, K), F32),
                jax.ShapeDtypeStruct((T, K), F32),
            ),
            in_specs=[whole] * 6,
            out_specs=(whole,) * 4,
            scratch_shapes=scratch,
            compiler_params=pltpu.CompilerParams(
                collective_id=0, has_side_effects=True, vmem_limit_bytes=56 * 2**20
            ),
        )(inner_acts, out_grad, write_proj, read_proj, log_decay, w_in)

    return jax.shard_map(
        local,
        mesh=mesh,
        in_specs=(
            P("seq", "head"),
            P("seq", "head"),
            P("seq", None),
            P("seq", None),
            P("seq", "head"),
            P("seq", "head"),
        ),
        out_specs=(P("seq", "head"), P("seq", "head"), P("seq", None), P("seq", None)),
        check_vma=False,
    )
```

```python
import functools

import jax
import jax.numpy as jnp
from jax import lax
from jax.experimental import pallas as pl
from jax.experimental.pallas import tpu as pltpu
from jax.sharding import PartitionSpec as P

MESH = pl.DeviceIdType.MESH
F32, BF16 = jnp.float32, jnp.bfloat16
Y = 4
T = 256
H = 8
K = 128
ROWS = 64

NN = (((1,), (0,)), ((), ()))
NT = (((1,), (1,)), ((), ()))
TN = (((0,), (0,)), ((), ()))


def dot(a, b, dims=NN):
    return lax.dot_general(a, b, dims, preferred_element_type=F32)


def remote(src, dst, send, recv, device):
    return pltpu.make_async_remote_copy(
        src, dst, send, recv, device_id=device, device_id_type=MESH
    )


def kernel(
    Z, X,
    x_ref, dy_ref, b_ref, c_ref, log_ref, w_ref,
    out_ref, act_ref, wg_ref, rg_ref,
    cs_ref, xs_ref, dys_ref, actl_ref, wt_ref,
    csall, ball, actl_all, tb_ref, atot,
    wz, up_s, up_r, dz_s, dz_r, zs, zr, cz, zin,
    g_s, g_r, st_s, st_r, act_all,
    co_s, co_r, keep, x_s, x_r, y_s, y_r,
    p_s, p_r, px, pf, pf_r, part_ref,
    y_ss, y_rs, w_ss, w_rs, z_ss, z_rs, c_ss, c_rs, x_ss, x_rs, a_ss, a_rs, known,
):
    seq, head = lax.axis_index("seq"), lax.axis_index("head")
    z, y = seq // Y, lax.rem(seq, Y)
    cx, core = head // 2, lax.rem(head, 2)

    def at_z(d):
        return (lax.rem(z + d + Z, Z) * Y + y, head)

    def y_of(d):
        return lax.rem(y + d + Y, Y)

    def at_y(d):
        return (z * Y + y_of(d), head)

    def x_of(d):
        return lax.rem(cx + d + X, X)

    def at_x(d):
        return (seq, x_of(d) * 2 + core)

    other = (seq, cx * 2 + 1 - core)

    barrier = pltpu.get_barrier_semaphore()
    partners = (
        [at_y(d) for d in range(1, Y)]
        + [at_x(d) for d in range(1, X)]
        + [other, at_z(1), at_z(-1)]
    )
    for device in partners:
        pl.semaphore_signal(barrier, inc=1, device_id=device, device_id_type=MESH)

    rows = lax.broadcasted_iota(jnp.int32, (T, T), 0)
    lanes = lax.broadcasted_iota(jnp.int32, (T, T), 1)
    upper = jnp.where(rows <= lanes, 1.0, 0.0).astype(F32)
    cs_rows = lax.dot_general(
        log_ref[...], upper, NN, precision=lax.Precision.HIGHEST, preferred_element_type=F32
    )
    cs = jnp.concatenate([cs_rows, jnp.zeros((K - H, T), F32)], axis=0).T
    cs_ref[...] = cs
    csall[y] = cs_rows
    ball[y] = b_ref[...]
    wz[z] = w_ref[...]
    tail = jnp.exp(cs[T - 1 : T] - cs)
    front = jnp.exp(cs)
    for h in range(H):
        cut = slice(h * K, (h + 1) * K)
        xs_ref[:, cut] = (x_ref[:, cut].astype(F32) * tail[:, h : h + 1]).astype(BF16)
        dys_ref[:, cut] = (dy_ref[:, cut].astype(F32) * front[:, h : h + 1]).astype(BF16)
    for i, (left, right) in enumerate(((b_ref, xs_ref), (c_ref, dys_ref))):
        total = dot(left[...], right[...], TN).astype(BF16)
        for h in range(H):
            up_s[i, h // 2, (h % 2) * K : (h % 2 + 1) * K] = total[:, h * K : (h + 1) * K]
    for i in range(2):
        up_r[i, y] = up_s[i, y]

    pl.semaphore_wait(barrier, len(partners))

    def tell(k):
        for d in (1 << k, -(1 << k)):
            pl.semaphore_signal(known.at[k], inc=1, device_id=at_z(d), device_id_type=MESH)

    def told(k):
        pl.semaphore_wait(known.at[k], 2)

    rounds = (Z // 2 - 1).bit_length()
    tell(0)

    half = Z // 2

    steps = [(part, side) for part in range(2) for side in range(2)]

    def w_copy(k, part, side, block):
        here = wz.at[block, part * (ROWS // 2) : (part + 1) * (ROWS // 2)]
        return remote(
            here, here, w_ss.at[side, k, part], w_rs.at[side, k, part], at_z(1 - 2 * side)
        )

    def w_sent(k, part, side):
        return w_copy(k, part, side, lax.rem(z + (2 * side - 1) * k + Z, Z))

    def w_arrived(k, part, side):
        w_copy(k, part, side, lax.rem(z + (2 * side - 1) * (k + 1) + Z, Z)).wait_recv()

    def w_steps(k):
        return [step for step in steps if k < half - 1 or step[0] == step[1]]

    def w_step(k):
        for step in steps:
            if k > 0:
                w_arrived(k - 1, *step)
            if step in w_steps(k):
                w_sent(k, *step).start()

    started = []

    def y_send(group, src_of, dst_of):
        for d in (2, 1, 3):
            copy = remote(
                src_of(y_of(d)), dst_of(y), y_ss.at[group, d], y_rs.at[group, d], at_y(d)
            )
            copy.start()
            started.append(copy)

    def y_wait(group, src_of, dst_of):
        for d in (1, 3, 2):
            remote(
                src_of(y_of(d)), dst_of(y_of(-d)), y_ss.at[group, d], y_rs.at[group, d], at_y(d)
            ).wait_recv()

    def cs_of(t):
        return csall.at[y]

    def up_of(i):
        return lambda t: up_s.at[i, t], lambda s: up_r.at[i, s]

    y_send(0, cs_of, lambda s: csall.at[s])
    y_send(1, *up_of(1))
    w_step(0)

    below = lanes >= rows
    scores = dot(b_ref[...], c_ref[...], NT)

    def heads(low, high):
        for h in range(low, high):
            cut = slice(h * K, (h + 1) * K)
            xh, dyh = x_ref[:, cut], dy_ref[:, cut]
            decay = jnp.exp(
                jnp.where(below, csall[y, h : h + 1, :] - cs_ref[:, h : h + 1], -jnp.inf)
            )
            weighted = decay * dot(xh, dyh, NT)
            wt_ref[...] = weighted if h == 0 else wt_ref[...] + weighted
            own = dot((decay * scores).astype(BF16), dyh)
            actl_ref[:, cut] = own
            actl_all[y, h // 4, :, (h % 4) * K : (h % 4 + 1) * K] = own.astype(BF16)

    def act_copy(part, side):
        block = actl_all.at[y, part]
        return remote(block, block, a_ss.at[part, side], a_rs.at[part, side], at_y(1 - 2 * side))

    def act_arrived(part, side):
        block = actl_all.at[y_of(2 * side - 1), part]
        remote(block, block, a_ss.at[part, side], a_rs.at[part, side], at_y(1 - 2 * side)).wait_recv()

    def act_relay(part):
        block = actl_all.at[y_of(2 * part - 1), part]
        return remote(block, block, a_ss.at[2, part], a_rs.at[2, part], at_y(1 - 2 * part))

    def act_relayed(part):
        block = actl_all.at[y_of(2), part]
        remote(block, block, a_ss.at[2, part], a_rs.at[2, part], at_y(1 - 2 * part)).wait_recv()

    def total_of(t, i):
        return atot[t, pl.ds(2 * y + i, 1), :]

    def z_send(group, src_of, dst):
        def one(d, carry):
            t = lax.rem(z + d, Z)
            remote(
                src_of(t), dst.at[z], z_ss.at[group, d], z_rs.at[group, d], at_z(d)
            ).start()
            return carry

        lax.fori_loop(1, Z, one, 0)

    def z_wait(group, src_of, dst):
        def one(d, carry):
            remote(
                src_of(lax.rem(z + d, Z)), dst.at[lax.rem(z - d + Z, Z)],
                z_ss.at[group, d], z_rs.at[group, d], at_z(d),
            ).wait_recv()
            return carry

        lax.fori_loop(1, Z, one, 0)

    def z_sent(group, src_of, dst):
        def one(d, carry):
            remote(
                src_of(lax.rem(z + d, Z)), dst.at[z],
                z_ss.at[group, d], z_rs.at[group, d], at_z(d),
            ).wait_send()
            return carry

        lax.fori_loop(1, Z, one, 0)

    def dz_of(t):
        return dz_s.at[t // (Z // 2)]

    def z_up(i):
        return 1 + i, lambda t: zs.at[i, t], zr.at[i]

    def z_down(i):
        return 3 + i, lambda t: cz.at[i, t], zin.at[i]

    def plane_totals(i):
        for n in range(2):
            cut = slice(n * K, (n + 1) * K)
            spans = range(Y) if i == 0 else range(Y - 1, -1, -1)
            total = None
            for t in spans:
                own = up_r[i, t, cut].astype(F32)
                total = own if total is None else jnp.exp(total_of(t, n)) * total + own
            zs[i, n * (Z // 2) : (n + 1) * (Z // 2)] = total.astype(BF16).reshape(
                Z // 2, 2 * K // Z, K
            )
        zr[i, z] = zs[i, z]

    def sweep(i):
        def one(k, total):
            j = k if i == 0 else Z - 1 - k
            cz[i, j] = total.astype(BF16)
            return jnp.exp(dz_r[j]) * total + zr[i, j].astype(F32)

        lax.fori_loop(0, Z, one, jnp.zeros((2 * K // Z, K), F32))
        zin[i, z] = cz[i, z]

    def carry_in(i, dst):
        for n in range(2):
            cut = slice(n * K, (n + 1) * K)
            total = zin[i, n * (Z // 2) : (n + 1) * (Z // 2)].reshape(K, K).astype(F32)
            for t in range(Y) if i == 0 else range(Y - 1, -1, -1):
                dst[t, cut] = total.astype(BF16)
                total = jnp.exp(total_of(t, n)) * total + up_r[i, t, cut].astype(F32)

    heads(0, 2)
    for k in range(1, rounds):
        told(k - 1)
        tell(k)
    heads(2, 4)
    w_step(1)
    y_wait(0, cs_of, lambda s: csall.at[s])
    for t in range(Y):
        atot[t] = jnp.broadcast_to(csall[t][:, T - 1 : T], (H, K))
    for i in range(2):
        plane = total_of(0, i) + total_of(1, i) + total_of(2, i) + total_of(3, i)
        dz_s[i] = plane
    dz_r[z] = dz_s[z // (Z // 2)]
    told(rounds - 1)
    z_send(0, dz_of, dz_r)

    y_wait(1, *up_of(1))
    plane_totals(1)
    z_send(*z_up(1))
    y_send(3, *up_of(0))
    y_send(2, lambda t: ball.at[y], lambda s: ball.at[s])
    act_copy(0, 0).start()
    act_copy(0, 1).start()
    w_step(2)
    heads(4, 8)
    act_copy(1, 0).start()
    act_copy(1, 1).start()
    w_step(3)

    y_wait(3, *up_of(0))
    plane_totals(0)
    z_wait(0, dz_of, dz_r)
    z_wait(*z_up(1))
    sweep(1)
    z_send(*z_down(1))
    z_send(*z_up(0))
    w_step(4)

    y_wait(2, lambda t: ball.at[y], lambda s: ball.at[s])

    def tails(t, carry):
        padded = jnp.concatenate([csall[t], jnp.zeros((K - H, T), F32)], axis=0)
        ct = padded.T
        et = jnp.exp(ct[T - 1 : T] - ct)
        bt = ball[t].astype(F32)
        for h in range(H):
            tb_ref[t, h] = (et[:, h : h + 1] * bt).astype(BF16)
        return carry

    lax.fori_loop(0, Y, tails, 0)
    act_arrived(0, 0)
    act_relay(0).start()
    w_step(5)

    z_wait(*z_down(1))
    carry_in(1, g_s)
    g_r[y] = g_s[...]
    order = (1, 3, 2, 0)

    def grad_copy(k, e):
        t = y_of(e + order[k])
        return remote(g_s.at[t], g_r.at[y, t], y_ss.at[4 + k, e], y_rs.at[4 + k, e], at_y(e))

    def grad_wait(k):
        t = y_of(order[k])
        for e in (1, 3, 2):
            remote(
                g_s.at[t], g_r.at[y_of(-e), t], y_ss.at[4 + k, e], y_rs.at[4 + k, e], at_y(e)
            ).wait_recv()

    def grad_start(k):
        for e in (2, 1, 3):
            grad_copy(k, e).start()

    grad_start(0)
    grad_start(1)
    act_arrived(1, 1)
    act_relay(1).start()
    grad_start(2)
    grad_start(3)
    w_step(6)
    z_wait(*z_up(0))
    sweep(0)
    z_send(*z_down(0))
    w_step(7)
    wt = wt_ref[...]
    part_ref[0] = dot(wt.astype(BF16), c_ref[...])
    part_ref[1] = dot(wt.T.astype(BF16), b_ref[...])

    def core_copy(k):
        return remote(co_s.at[k], co_r.at[k], c_ss.at[k], c_rs.at[k], other)

    def stage_a(k):
        d = order[k]
        t = y_of(d)
        grad_wait(k)
        for h in range(H):
            cut = slice(h * K, (h + 1) * K)
            carried = dot(tb_ref[t, h], g_r[h // 2, t, (h % 2) * K : (h % 2 + 1) * K])
            if d == 0:
                own = (actl_ref[:, cut] + carried).astype(BF16)
                act_ref[:, cut] = own
            else:
                local = actl_all[t, h // 4, :, (h % 4) * K : (h % 4 + 1) * K]
                own = (local.astype(F32) + carried).astype(BF16)
            act_all[k, :, cut] = own
        if k == 0:
            for step in w_steps(half - 1):
                w_arrived(half - 1, *step)
        act = act_all[k]
        per = Z // X
        for j in range(X):
            w = wz[per * j : per * (j + 1)].reshape(per * ROWS, H * K)
            both = dot(act, w, NT)
            low, high = both[:, 0:K], both[:, K : 2 * K]
            keep[k, j] = jnp.where(core == 0, low, high)
            co_s[k, j] = jnp.where(core == 0, high, low).astype(BF16)
        core_copy(k).start()

    def x_copies(k):
        return [
            remote(
                x_s.at[k, x_of(e)], x_r.at[k, e], x_ss.at[k, e], x_rs.at[k, e], at_x(e)
            )
            for e in range(1, X)
        ]

    def stage_b(k):
        core_copy(k).wait_recv()
        for j in range(X):
            total = keep[k, j] + co_r[k, j].astype(F32)
            keep[k, j] = total
            x_s[k, j] = total.astype(BF16)
        for copy in x_copies(k):
            copy.start()

    def y_copy(k):
        d = order[k]
        return remote(y_s.at[k], y_r.at[y], y_ss.at[9, d], y_rs.at[9, d], at_y(d))

    def stage_c(k):
        total = keep[k, cx]
        for e, copy in enumerate(x_copies(k), 1):
            copy.wait_recv()
            total = total + x_r[k, e].astype(F32)
        if order[k] == 0:
            y_r[y] = total.astype(BF16)
        else:
            y_s[k] = total.astype(BF16)
            y_copy(k).start()

    core_part = remote(p_s, p_r, c_ss.at[4], c_rs.at[4], other)
    core_total = remote(pf, pf_r, c_ss.at[5], c_rs.at[5], other)

    def parts_start():
        state = [st_r[h // 2, (h % 2) * K : (h % 2 + 1) * K] for h in range(H)]
        grad = [g_r[h // 2, y, (h % 2) * K : (h % 2 + 1) * K] for h in range(H)]
        write = part_ref[0] + dot(xs_ref[...], jnp.concatenate(grad, axis=1), NT)
        read = part_ref[1] + dot(dys_ref[...], jnp.concatenate(state, axis=1), NT)
        part_ref[0] = jnp.where(core == 0, write, read)
        p_s[...] = jnp.where(core == 0, read, write).astype(BF16)
        core_part.start()

    def part_copy(e):
        return remote(px.at[cx], px.at[cx], x_ss.at[4, e], x_rs.at[4, e], at_x(e))

    def parts_x():
        core_part.wait_recv()
        px[cx] = (part_ref[0] + p_r[...].astype(F32)).astype(BF16)
        for e in range(1, X):
            part_copy(e).start()

    def parts_core():
        for e in range(1, X):
            s = x_of(-e)
            remote(px.at[cx], px.at[s], x_ss.at[4, e], x_rs.at[4, e], at_x(e)).wait_recv()
        total = px[0].astype(F32)
        for j in range(1, X):
            total = total + px[j].astype(F32)
        pf[...] = total
        core_total.start()

    def state_of(t):
        return st_s.at[t]

    def states():
        z_wait(*z_down(0))
        carry_in(0, st_s)
        st_r[y] = st_s[y]
        y_send(8, state_of, lambda s: st_r.at[s])

    act_arrived(0, 1)
    stage_a(0)
    act_arrived(1, 0)
    stage_a(1)
    stage_b(0)
    states()
    act_relayed(0)
    act_relayed(1)
    stage_a(2)
    stage_b(1)
    stage_c(0)
    stage_a(3)
    stage_b(2)
    y_wait(8, state_of, lambda s: st_r.at[s])
    parts_start()
    stage_c(1)
    stage_b(3)
    parts_x()
    stage_c(2)
    parts_core()
    stage_c(3)
    core_total.wait_recv()
    wg_ref[...] = jnp.where(core == 0, pf[...], pf_r[...])
    rg_ref[...] = jnp.where(core == 0, pf_r[...], pf[...])
    for k in range(3):
        d = order[k]
        remote(
            y_s.at[k], y_r.at[y_of(-d)], y_ss.at[9, d], y_rs.at[9, d], at_y(d)
        ).wait_recv()
    for i in range(2):
        pieces = [y_r[t, :, i * ROWS : (i + 1) * ROWS] for t in range(Y)]
        out_ref[:, 2 * i * K : 2 * (i + 1) * K] = jnp.concatenate(pieces, axis=1)

    for copy in started:
        copy.wait_send()
    for k in range(half):
        for step in w_steps(k):
            w_sent(k, *step).wait_send()
    z_sent(0, dz_of, dz_r)
    for i in range(2):
        z_sent(*z_up(i))
        z_sent(*z_down(i))
        act_copy(i, 0).wait_send()
        act_copy(i, 1).wait_send()
        act_relay(i).wait_send()
    for k in range(4):
        for e in range(1, Y):
            grad_copy(k, e).wait_send()
    for k in range(4):
        core_copy(k).wait_send()
        for copy in x_copies(k):
            copy.wait_send()
        if order[k]:
            y_copy(k).wait_send()
    core_part.wait_send()
    core_total.wait_send()
    for e in range(1, X):
        part_copy(e).wait_send()


def solution(mesh):
    Z, X = mesh.shape["seq"] // Y, mesh.shape["head"] // 2
    piece = 2 * K // Z
    vmem, dma = pltpu.VMEM, pltpu.SemaphoreType.DMA

    def local(inner_acts, out_grad, write_proj, read_proj, log_decay, w_in):
        scratch = [
            vmem((T, K), F32),
            vmem((T, H * K), BF16),
            vmem((T, H * K), BF16),
            vmem((T, H * K), F32),
            vmem((T, T), F32),
            vmem((Y, H, T), F32),
            vmem((Y, T, K), BF16),
            vmem((Y, 2, T, H * K // 2), BF16),
            vmem((Y, H, T, K), BF16),
            vmem((Y, H, K), F32),
            vmem((Z, ROWS, H * K), BF16),
            vmem((2, Y, 2 * K, K), BF16),
            vmem((2, Y, 2 * K, K), BF16),
            vmem((2, 1, K), F32),
            vmem((Z, 1, K), F32),
            vmem((2, Z, piece, K), BF16),
            vmem((2, Z, piece, K), BF16),
            vmem((2, Z, piece, K), BF16),
            vmem((2, Z, piece, K), BF16),
            vmem((Y, 2 * K, K), BF16),
            vmem((Y, Y, 2 * K, K), BF16),
            vmem((Y, 2 * K, K), BF16),
            vmem((Y, 2 * K, K), BF16),
            vmem((Y, T, H * K), BF16),
            vmem((Y, X, T, K), BF16),
            vmem((Y, X, T, K), BF16),
            vmem((Y, X, T, K), F32),
            vmem((Y, X, T, K), BF16),
            vmem((Y, X, T, K), BF16),
            vmem((Y, T, K), BF16),
            vmem((Y, T, K), BF16),
            vmem((T, K), BF16),
            vmem((T, K), BF16),
            vmem((X, T, K), BF16),
            vmem((T, K), F32),
            vmem((T, K), F32),
            vmem((2, T, K), F32),
            dma((10, Y)), dma((10, Y)),
            dma((2, Z // 2, 2)), dma((2, Z // 2, 2)),
            dma((5, Z)), dma((5, Z)),
            dma((6,)), dma((6,)),
            dma((5, X)), dma((5, X)),
            dma((3, 2)), dma((3, 2)),
            pltpu.SemaphoreType.REGULAR(((Z // 2 - 1).bit_length(),)),
        ]
        whole = pl.BlockSpec(memory_space=pltpu.VMEM)
        columns = w_in.shape[0] * mesh.shape["seq"] // mesh.shape["head"]
        return pl.pallas_call(
            functools.partial(kernel, Z, X),
            out_shape=(
                jax.ShapeDtypeStruct((T, columns), BF16),
                jax.ShapeDtypeStruct((T, H * K), BF16),
                jax.ShapeDtypeStruct((T, K), F32),
                jax.ShapeDtypeStruct((T, K), F32),
            ),
            in_specs=[whole] * 6,
            out_specs=(whole,) * 4,
            scratch_shapes=scratch,
            compiler_params=pltpu.CompilerParams(
                collective_id=0, has_side_effects=True, vmem_limit_bytes=56 * 2**20
            ),
        )(inner_acts, out_grad, write_proj, read_proj, log_decay.T, w_in)

    return jax.shard_map(
        local,
        mesh=mesh,
        in_specs=(
            P("seq", "head"),
            P("seq", "head"),
            P("seq", None),
            P("seq", None),
            P("seq", "head"),
            P("seq", "head"),
        ),
        out_specs=(P("seq", "head"), P("seq", "head"), P("seq", None), P("seq", None)),
        check_vma=False,
    )
```

```python
import functools

import jax
import jax.numpy as jnp
from jax import lax
from jax.experimental import pallas as pl
from jax.experimental.pallas import tpu as pltpu
from jax.sharding import PartitionSpec as P

MESH = pl.DeviceIdType.MESH
F32, BF16 = jnp.float32, jnp.bfloat16
Y = 4
T = 256
H = 8
K = 128
ROWS = 64

NN = (((1,), (0,)), ((), ()))
NT = (((1,), (1,)), ((), ()))
TN = (((0,), (0,)), ((), ()))


def dot(a, b, dims=NN):
    return lax.dot_general(a, b, dims, preferred_element_type=F32)


def remote(src, dst, send, recv, device):
    return pltpu.make_async_remote_copy(
        src, dst, send, recv, device_id=device, device_id_type=MESH
    )


def kernel(
    Z, X,
    x_in, dy_in, b_ref, c_ref, log_ref, w_in,
    out_ref, act_ref, wg_ref, rg_ref,
    x_ref, dy_ref, w_ref, cs_ref, xs_ref, dys_ref, actl_ref, wt_ref,
    csall, ball, actl_all, tb_ref, atot,
    wz, up_s, up_r, dz_s, dz_r, zs, zr, cz, zin,
    g_s, g_r, st_s, st_r, act_all,
    co_s, co_r, keep, x_s, x_r, y_s, y_r,
    p_s, p_r, px, pf, pf_r, part_ref,
    y_ss, y_rs, w_ss, w_rs, z_ss, z_rs, c_ss, c_rs, x_ss, x_rs, a_ss, a_rs, known, loaded,
):
    seq, head = lax.axis_index("seq"), lax.axis_index("head")
    z, y = seq // Y, lax.rem(seq, Y)
    cx, core = head // 2, lax.rem(head, 2)

    def at_z(d):
        return (lax.rem(z + d + Z, Z) * Y + y, head)

    def y_of(d):
        return lax.rem(y + d + Y, Y)

    def at_y(d):
        return (z * Y + y_of(d), head)

    def x_of(d):
        return lax.rem(cx + d + X, X)

    def at_x(d):
        return (seq, x_of(d) * 2 + core)

    other = (seq, cx * 2 + 1 - core)

    loads = [
        pltpu.make_async_copy(src, dst, loaded.at[i])
        for i, (src, dst) in enumerate(((x_in, x_ref), (dy_in, dy_ref), (w_in, w_ref)))
    ]
    for copy in loads:
        copy.start()

    barrier = pltpu.get_barrier_semaphore()
    partners = (
        [at_y(d) for d in range(1, Y)]
        + [at_x(d) for d in range(1, X)]
        + [other, at_z(1), at_z(-1)]
    )
    for device in partners:
        pl.semaphore_signal(barrier, inc=1, device_id=device, device_id_type=MESH)

    rows = lax.broadcasted_iota(jnp.int32, (T, T), 0)
    lanes = lax.broadcasted_iota(jnp.int32, (T, T), 1)
    upper = jnp.where(rows <= lanes, 1.0, 0.0).astype(F32)
    cs_rows = lax.dot_general(
        log_ref[...], upper, NN, precision=lax.Precision.HIGHEST, preferred_element_type=F32
    )
    cs = jnp.concatenate([cs_rows, jnp.zeros((K - H, T), F32)], axis=0).T
    cs_ref[...] = cs
    csall[y] = cs_rows
    ball[y] = b_ref[...]
    tail = jnp.exp(cs[T - 1 : T] - cs)
    front = jnp.exp(cs)
    for copy in loads:
        copy.wait()
    wz[z] = w_ref[...]
    for h in range(H):
        cut = slice(h * K, (h + 1) * K)
        xs_ref[:, cut] = (x_ref[:, cut].astype(F32) * tail[:, h : h + 1]).astype(BF16)
        dys_ref[:, cut] = (dy_ref[:, cut].astype(F32) * front[:, h : h + 1]).astype(BF16)
    for i, (left, right) in enumerate(((b_ref, xs_ref), (c_ref, dys_ref))):
        total = dot(left[...], right[...], TN).astype(BF16)
        for h in range(H):
            up_s[i, h // 2, (h % 2) * K : (h % 2 + 1) * K] = total[:, h * K : (h + 1) * K]
    for i in range(2):
        up_r[i, y] = up_s[i, y]

    pl.semaphore_wait(barrier, len(partners))

    def tell(k):
        for d in (1 << k, -(1 << k)):
            pl.semaphore_signal(known.at[k], inc=1, device_id=at_z(d), device_id_type=MESH)

    def told(k):
        pl.semaphore_wait(known.at[k], 2)

    rounds = (Z // 2 - 1).bit_length()
    tell(0)

    half = Z // 2

    steps = [(part, side) for part in range(2) for side in range(2)]

    def w_copy(k, part, side, block):
        here = wz.at[block, part * (ROWS // 2) : (part + 1) * (ROWS // 2)]
        return remote(
            here, here, w_ss.at[side, k, part], w_rs.at[side, k, part], at_z(1 - 2 * side)
        )

    def w_sent(k, part, side):
        return w_copy(k, part, side, lax.rem(z + (2 * side - 1) * k + Z, Z))

    def w_arrived(k, part, side):
        w_copy(k, part, side, lax.rem(z + (2 * side - 1) * (k + 1) + Z, Z)).wait_recv()

    def w_steps(k):
        return [step for step in steps if k < half - 1 or step[0] == step[1]]

    def w_step(k):
        for step in steps:
            if k > 0:
                w_arrived(k - 1, *step)
            if step in w_steps(k):
                w_sent(k, *step).start()

    started = []

    def y_send(group, src_of, dst_of):
        for d in (2, 1, 3):
            copy = remote(
                src_of(y_of(d)), dst_of(y), y_ss.at[group, d], y_rs.at[group, d], at_y(d)
            )
            copy.start()
            started.append(copy)

    def y_wait(group, src_of, dst_of):
        for d in (1, 3, 2):
            remote(
                src_of(y_of(d)), dst_of(y_of(-d)), y_ss.at[group, d], y_rs.at[group, d], at_y(d)
            ).wait_recv()

    def cs_of(t):
        return csall.at[y]

    def up_of(i):
        return lambda t: up_s.at[i, t], lambda s: up_r.at[i, s]

    y_send(0, cs_of, lambda s: csall.at[s])
    y_send(1, *up_of(1))
    w_step(0)

    below = lanes >= rows
    scores = dot(b_ref[...], c_ref[...], NT)

    def heads(low, high):
        for h in range(low, high):
            cut = slice(h * K, (h + 1) * K)
            xh, dyh = x_ref[:, cut], dy_ref[:, cut]
            decay = jnp.exp(
                jnp.where(below, csall[y, h : h + 1, :] - cs_ref[:, h : h + 1], -jnp.inf)
            )
            weighted = decay * dot(xh, dyh, NT)
            wt_ref[...] = weighted if h == 0 else wt_ref[...] + weighted
            own = dot((decay * scores).astype(BF16), dyh)
            actl_ref[:, cut] = own
            actl_all[y, h // 4, :, (h % 4) * K : (h % 4 + 1) * K] = own.astype(BF16)

    def act_copy(part, side):
        block = actl_all.at[y, part]
        return remote(block, block, a_ss.at[part, side], a_rs.at[part, side], at_y(1 - 2 * side))

    def act_arrived(part, side):
        block = actl_all.at[y_of(2 * side - 1), part]
        remote(block, block, a_ss.at[part, side], a_rs.at[part, side], at_y(1 - 2 * side)).wait_recv()

    def act_relay(part):
        block = actl_all.at[y_of(2 * part - 1), part]
        return remote(block, block, a_ss.at[2, part], a_rs.at[2, part], at_y(1 - 2 * part))

    def act_relayed(part):
        block = actl_all.at[y_of(2), part]
        remote(block, block, a_ss.at[2, part], a_rs.at[2, part], at_y(1 - 2 * part)).wait_recv()

    def total_of(t, i):
        return atot[t, pl.ds(2 * y + i, 1), :]

    def z_send(group, src_of, dst):
        def one(d, carry):
            t = lax.rem(z + d, Z)
            remote(
                src_of(t), dst.at[z], z_ss.at[group, d], z_rs.at[group, d], at_z(d)
            ).start()
            return carry

        lax.fori_loop(1, Z, one, 0)

    def z_wait(group, src_of, dst):
        def one(d, carry):
            remote(
                src_of(lax.rem(z + d, Z)), dst.at[lax.rem(z - d + Z, Z)],
                z_ss.at[group, d], z_rs.at[group, d], at_z(d),
            ).wait_recv()
            return carry

        lax.fori_loop(1, Z, one, 0)

    def z_sent(group, src_of, dst):
        def one(d, carry):
            remote(
                src_of(lax.rem(z + d, Z)), dst.at[z],
                z_ss.at[group, d], z_rs.at[group, d], at_z(d),
            ).wait_send()
            return carry

        lax.fori_loop(1, Z, one, 0)

    def dz_of(t):
        return dz_s.at[t // (Z // 2)]

    def z_up(i):
        return 1 + i, lambda t: zs.at[i, t], zr.at[i]

    def z_down(i):
        return 3 + i, lambda t: cz.at[i, t], zin.at[i]

    def plane_totals(i):
        for n in range(2):
            cut = slice(n * K, (n + 1) * K)
            spans = range(Y) if i == 0 else range(Y - 1, -1, -1)
            total = None
            for t in spans:
                own = up_r[i, t, cut].astype(F32)
                total = own if total is None else jnp.exp(total_of(t, n)) * total + own
            zs[i, n * (Z // 2) : (n + 1) * (Z // 2)] = total.astype(BF16).reshape(
                Z // 2, 2 * K // Z, K
            )
        zr[i, z] = zs[i, z]

    def sweep(i):
        def one(k, total):
            j = k if i == 0 else Z - 1 - k
            cz[i, j] = total.astype(BF16)
            return jnp.exp(dz_r[j]) * total + zr[i, j].astype(F32)

        lax.fori_loop(0, Z, one, jnp.zeros((2 * K // Z, K), F32))
        zin[i, z] = cz[i, z]

    def carry_in(i, dst):
        for n in range(2):
            cut = slice(n * K, (n + 1) * K)
            total = zin[i, n * (Z // 2) : (n + 1) * (Z // 2)].reshape(K, K).astype(F32)
            for t in range(Y) if i == 0 else range(Y - 1, -1, -1):
                dst[t, cut] = total.astype(BF16)
                total = jnp.exp(total_of(t, n)) * total + up_r[i, t, cut].astype(F32)

    heads(0, 2)
    for k in range(1, rounds):
        told(k - 1)
        tell(k)
    heads(2, 4)
    w_step(1)
    y_wait(0, cs_of, lambda s: csall.at[s])
    for t in range(Y):
        atot[t] = jnp.broadcast_to(csall[t][:, T - 1 : T], (H, K))
    for i in range(2):
        plane = total_of(0, i) + total_of(1, i) + total_of(2, i) + total_of(3, i)
        dz_s[i] = plane
    dz_r[z] = dz_s[z // (Z // 2)]
    told(rounds - 1)
    z_send(0, dz_of, dz_r)

    y_wait(1, *up_of(1))
    plane_totals(1)
    z_send(*z_up(1))
    y_send(3, *up_of(0))
    y_send(2, lambda t: ball.at[y], lambda s: ball.at[s])
    act_copy(0, 0).start()
    act_copy(0, 1).start()
    w_step(2)
    heads(4, 8)
    act_copy(1, 0).start()
    act_copy(1, 1).start()
    w_step(3)

    y_wait(3, *up_of(0))
    plane_totals(0)
    z_wait(0, dz_of, dz_r)
    z_wait(*z_up(1))
    sweep(1)
    z_send(*z_down(1))
    z_send(*z_up(0))
    w_step(4)

    y_wait(2, lambda t: ball.at[y], lambda s: ball.at[s])

    def tails(t, carry):
        padded = jnp.concatenate([csall[t], jnp.zeros((K - H, T), F32)], axis=0)
        ct = padded.T
        et = jnp.exp(ct[T - 1 : T] - ct)
        bt = ball[t].astype(F32)
        for h in range(H):
            tb_ref[t, h] = (et[:, h : h + 1] * bt).astype(BF16)
        return carry

    lax.fori_loop(0, Y, tails, 0)
    act_arrived(0, 0)
    act_relay(0).start()
    w_step(5)

    z_wait(*z_down(1))
    carry_in(1, g_s)
    g_r[y] = g_s[...]
    order = (1, 3, 2, 0)

    def grad_copy(k, e):
        t = y_of(e + order[k])
        return remote(g_s.at[t], g_r.at[y, t], y_ss.at[4 + k, e], y_rs.at[4 + k, e], at_y(e))

    def grad_wait(k):
        t = y_of(order[k])
        for e in (1, 3, 2):
            remote(
                g_s.at[t], g_r.at[y_of(-e), t], y_ss.at[4 + k, e], y_rs.at[4 + k, e], at_y(e)
            ).wait_recv()

    def grad_start(k):
        for e in (2, 1, 3):
            grad_copy(k, e).start()

    grad_start(0)
    grad_start(1)
    act_arrived(1, 1)
    act_relay(1).start()
    grad_start(2)
    grad_start(3)
    w_step(6)
    z_wait(*z_up(0))
    sweep(0)
    z_send(*z_down(0))
    w_step(7)
    wt = wt_ref[...]
    part_ref[0] = dot(wt.astype(BF16), c_ref[...])
    part_ref[1] = dot(wt.T.astype(BF16), b_ref[...])

    def core_copy(k):
        return remote(co_s.at[k], co_r.at[k], c_ss.at[k], c_rs.at[k], other)

    def stage_a(k):
        d = order[k]
        t = y_of(d)
        grad_wait(k)
        for h in range(H):
            cut = slice(h * K, (h + 1) * K)
            carried = dot(tb_ref[t, h], g_r[h // 2, t, (h % 2) * K : (h % 2 + 1) * K])
            if d == 0:
                own = (actl_ref[:, cut] + carried).astype(BF16)
                act_ref[:, cut] = own
            else:
                local = actl_all[t, h // 4, :, (h % 4) * K : (h % 4 + 1) * K]
                own = (local.astype(F32) + carried).astype(BF16)
            act_all[k, :, cut] = own
        if k == 0:
            for step in w_steps(half - 1):
                w_arrived(half - 1, *step)
        act = act_all[k]
        per = Z // X
        for j in range(X):
            w = wz[per * j : per * (j + 1)].reshape(per * ROWS, H * K)
            both = dot(act, w, NT)
            low, high = both[:, 0:K], both[:, K : 2 * K]
            keep[k, j] = jnp.where(core == 0, low, high)
            co_s[k, j] = jnp.where(core == 0, high, low).astype(BF16)
        core_copy(k).start()

    def x_copies(k):
        return [
            remote(
                x_s.at[k, x_of(e)], x_r.at[k, e], x_ss.at[k, e], x_rs.at[k, e], at_x(e)
            )
            for e in range(1, X)
        ]

    def stage_b(k):
        core_copy(k).wait_recv()
        for j in range(X):
            total = keep[k, j] + co_r[k, j].astype(F32)
            keep[k, j] = total
            x_s[k, j] = total.astype(BF16)
        for copy in x_copies(k):
            copy.start()

    def y_copy(k):
        d = order[k]
        return remote(y_s.at[k], y_r.at[y], y_ss.at[9, d], y_rs.at[9, d], at_y(d))

    def stage_c(k):
        total = keep[k, cx]
        for e, copy in enumerate(x_copies(k), 1):
            copy.wait_recv()
            total = total + x_r[k, e].astype(F32)
        if order[k] == 0:
            y_r[y] = total.astype(BF16)
        else:
            y_s[k] = total.astype(BF16)
            y_copy(k).start()

    core_part = remote(p_s, p_r, c_ss.at[4], c_rs.at[4], other)
    core_total = remote(pf, pf_r, c_ss.at[5], c_rs.at[5], other)

    def parts_start():
        state = [st_r[h // 2, (h % 2) * K : (h % 2 + 1) * K] for h in range(H)]
        grad = [g_r[h // 2, y, (h % 2) * K : (h % 2 + 1) * K] for h in range(H)]
        write = part_ref[0] + dot(xs_ref[...], jnp.concatenate(grad, axis=1), NT)
        read = part_ref[1] + dot(dys_ref[...], jnp.concatenate(state, axis=1), NT)
        part_ref[0] = jnp.where(core == 0, write, read)
        p_s[...] = jnp.where(core == 0, read, write).astype(BF16)
        core_part.start()

    def part_copy(e):
        return remote(px.at[cx], px.at[cx], x_ss.at[4, e], x_rs.at[4, e], at_x(e))

    def parts_x():
        core_part.wait_recv()
        px[cx] = (part_ref[0] + p_r[...].astype(F32)).astype(BF16)
        for e in range(1, X):
            part_copy(e).start()

    def parts_core():
        for e in range(1, X):
            s = x_of(-e)
            remote(px.at[cx], px.at[s], x_ss.at[4, e], x_rs.at[4, e], at_x(e)).wait_recv()
        total = px[0].astype(F32)
        for j in range(1, X):
            total = total + px[j].astype(F32)
        pf[...] = total
        core_total.start()

    def state_of(t):
        return st_s.at[t]

    def states():
        z_wait(*z_down(0))
        carry_in(0, st_s)
        st_r[y] = st_s[y]
        y_send(8, state_of, lambda s: st_r.at[s])

    act_arrived(0, 1)
    stage_a(0)
    act_arrived(1, 0)
    stage_a(1)
    stage_b(0)
    states()
    act_relayed(0)
    act_relayed(1)
    stage_a(2)
    stage_b(1)
    stage_c(0)
    stage_a(3)
    y_wait(8, state_of, lambda s: st_r.at[s])
    parts_start()
    stage_b(2)
    parts_x()
    stage_c(1)
    stage_b(3)

    for copy in started:
        copy.wait_send()
    for k in range(half):
        for step in w_steps(k):
            w_sent(k, *step).wait_send()
    z_sent(0, dz_of, dz_r)
    for i in range(2):
        z_sent(*z_up(i))
        z_sent(*z_down(i))
        act_copy(i, 0).wait_send()
        act_copy(i, 1).wait_send()
        act_relay(i).wait_send()
    for k in range(4):
        for e in range(1, Y):
            grad_copy(k, e).wait_send()

    stage_c(2)
    parts_core()
    stage_c(3)
    core_total.wait_recv()
    wg_ref[...] = jnp.where(core == 0, pf[...], pf_r[...])
    rg_ref[...] = jnp.where(core == 0, pf_r[...], pf[...])
    for k in range(3):
        d = order[k]
        remote(
            y_s.at[k], y_r.at[y_of(-d)], y_ss.at[9, d], y_rs.at[9, d], at_y(d)
        ).wait_recv()
    for i in range(2):
        pieces = [y_r[t, :, i * ROWS : (i + 1) * ROWS] for t in range(Y)]
        out_ref[:, 2 * i * K : 2 * (i + 1) * K] = jnp.concatenate(pieces, axis=1)

    for k in range(4):
        core_copy(k).wait_send()
        for copy in x_copies(k):
            copy.wait_send()
        if order[k]:
            y_copy(k).wait_send()
    core_part.wait_send()
    core_total.wait_send()
    for e in range(1, X):
        part_copy(e).wait_send()


def solution(mesh):
    Z, X = mesh.shape["seq"] // Y, mesh.shape["head"] // 2
    piece = 2 * K // Z
    vmem, dma = pltpu.VMEM, pltpu.SemaphoreType.DMA

    def local(inner_acts, out_grad, write_proj, read_proj, log_decay, w_in):
        scratch = [
            vmem((T, H * K), BF16),
            vmem((T, H * K), BF16),
            vmem((ROWS, H * K), BF16),
            vmem((T, K), F32),
            vmem((T, H * K), BF16),
            vmem((T, H * K), BF16),
            vmem((T, H * K), F32),
            vmem((T, T), F32),
            vmem((Y, H, T), F32),
            vmem((Y, T, K), BF16),
            vmem((Y, 2, T, H * K // 2), BF16),
            vmem((Y, H, T, K), BF16),
            vmem((Y, H, K), F32),
            vmem((Z, ROWS, H * K), BF16),
            vmem((2, Y, 2 * K, K), BF16),
            vmem((2, Y, 2 * K, K), BF16),
            vmem((2, 1, K), F32),
            vmem((Z, 1, K), F32),
            vmem((2, Z, piece, K), BF16),
            vmem((2, Z, piece, K), BF16),
            vmem((2, Z, piece, K), BF16),
            vmem((2, Z, piece, K), BF16),
            vmem((Y, 2 * K, K), BF16),
            vmem((Y, Y, 2 * K, K), BF16),
            vmem((Y, 2 * K, K), BF16),
            vmem((Y, 2 * K, K), BF16),
            vmem((Y, T, H * K), BF16),
            vmem((Y, X, T, K), BF16),
            vmem((Y, X, T, K), BF16),
            vmem((Y, X, T, K), F32),
            vmem((Y, X, T, K), BF16),
            vmem((Y, X, T, K), BF16),
            vmem((Y, T, K), BF16),
            vmem((Y, T, K), BF16),
            vmem((T, K), BF16),
            vmem((T, K), BF16),
            vmem((X, T, K), BF16),
            vmem((T, K), F32),
            vmem((T, K), F32),
            vmem((2, T, K), F32),
            dma((10, Y)), dma((10, Y)),
            dma((2, Z // 2, 2)), dma((2, Z // 2, 2)),
            dma((5, Z)), dma((5, Z)),
            dma((6,)), dma((6,)),
            dma((5, X)), dma((5, X)),
            dma((3, 2)), dma((3, 2)),
            pltpu.SemaphoreType.REGULAR(((Z // 2 - 1).bit_length(),)),
            dma((3,)),
        ]
        whole = pl.BlockSpec(memory_space=pltpu.VMEM)
        hbm = pl.BlockSpec(memory_space=pl.ANY)
        columns = w_in.shape[0] * mesh.shape["seq"] // mesh.shape["head"]
        return pl.pallas_call(
            functools.partial(kernel, Z, X),
            out_shape=(
                jax.ShapeDtypeStruct((T, columns), BF16),
                jax.ShapeDtypeStruct((T, H * K), BF16),
                jax.ShapeDtypeStruct((T, K), F32),
                jax.ShapeDtypeStruct((T, K), F32),
            ),
            in_specs=[hbm, hbm, whole, whole, whole, hbm],
            out_specs=(whole,) * 4,
            scratch_shapes=scratch,
            compiler_params=pltpu.CompilerParams(
                collective_id=0, has_side_effects=True, vmem_limit_bytes=56 * 2**20
            ),
        )(inner_acts, out_grad, write_proj, read_proj, log_decay.T, w_in)

    return jax.shard_map(
        local,
        mesh=mesh,
        in_specs=(
            P("seq", "head"),
            P("seq", "head"),
            P("seq", None),
            P("seq", None),
            P("seq", "head"),
            P("seq", "head"),
        ),
        out_specs=(P("seq", "head"), P("seq", "head"), P("seq", None), P("seq", None)),
        check_vma=False,
    )
```
